32 devices in a mesh: ctx: 8 (over y, x, core), exp: 4 (over z).
Axes of the slice: x: 2, y: 2, z: 4, core: 2. Of those that a mesh axis runs over, the one named last changes fastest.
Arguments:
- queries: bfloat16 [2048, 4096], P(('ctx', 'exp')), may hold values from -6 to 6
- rotated_key_heads: bfloat16 [2048, 512], P(('ctx', 'exp')), may hold values from -15 to 15
- stacked_value_heads: bfloat16 [2048, 512], P(('ctx', 'exp')), may hold values from -6 to 6
- moe_rows: bfloat16 [4096, 4096], P(('ctx', 'exp')), may hold values from -6 to 6
- expert_ids: int32 [4096, 8], P(('ctx', 'exp')), may hold values from 0 to 31, all different within a row; in each aligned block of 128 rows (0 to 127, 128 to 255, ...) at most 40 rows name the same one
- route_weights: float32 [4096, 8], P(('ctx', 'exp')), may hold values from 0.05 to 0.35
- w_gate: bfloat16 [32, 4096, 768], P(('ctx', 'exp')), may hold values from -0.09375 to 0.09375
- w_up: bfloat16 [32, 4096, 768], P(('ctx', 'exp')), may hold values from -0.09375 to 0.09375
- w_down: bfloat16 [32, 768, 4096], P(('ctx', 'exp')), may hold values from -0.21875 to 0.21875
Outputs:
- attended: bfloat16 [2048, 4096], P(('ctx', 'exp'))
- expert_mix: bfloat16 [4096, 4096], P(('ctx', 'exp'))
The draws below stay inside these ranges and needn't reach their ends.
Inputs may be any that keep to these rules, and one draw needn't show every extreme that they name: `expert_ids`: the 8 ids of a token are distinct. In each aligned block of 128 rows (the rows of one device) no expert is named by more than 40 rows, a bound that some block reaches.
All inputs are finite; a program needn't handle non-finite values.
Results may differ from the reference program's by a relative error of at most 0.0058.
Values may be sent and summed in bfloat16 or wider, within the bound.
No kernel may reach another device: no remote copies, remote signals or barrier semaphores. Data moves between devices by JAX's collectives and lax.ppermute only.
A program may use at most 192 MiB of HBM per device.

```python
import math
import jax
import jax.numpy as jnp
import numpy as np
from jax import lax

D = 4096
QUERY_HEADS = 32
KEY_VALUE_HEADS = 4
HEAD_WIDTH = 128
FFE = 768
TOPK = 8
MOE_TOK = 128
SEQUENCE_LENGTH = 2048
MOE_TOKENS = 4096
EXPERTS = 32
MOST = 40
N_CTX = 8
N_EXP = 4


def draw_queries(key, part):
    random_noise_key = jax.random.fold_in(key, 11)
    base_offset = jax.random.normal(random_noise_key, (SEQUENCE_LENGTH, QUERY_HEADS * HEAD_WIDTH), jnp.float32)
    return jnp.clip(base_offset, -6.0, 6.0).astype(jnp.bfloat16)


def draw_rotated_key_heads(key, part):
    random_noise_key = jax.random.fold_in(key, 12)
    base_offset = 2.5 * jax.random.normal(random_noise_key, (SEQUENCE_LENGTH, KEY_VALUE_HEADS * HEAD_WIDTH), jnp.float32)
    return jnp.clip(base_offset, -15.0, 15.0).astype(jnp.bfloat16)


def block_levels(rng, dims, cuts, low, top_value):
    gain, own = 1.0, jax.random.fold_in(rng, 6)
    for dim, shards_of in cuts:
        heights = jnp.exp(jax.random.uniform(jax.random.fold_in(own, dim), (shards_of,), jnp.float32, low / len(cuts), top_value / len(cuts)))
        gain = gain * jnp.repeat(heights, dims[dim] // shards_of).reshape([-1 if axis == dim else 1 for axis in range(len(dims))])
    return gain


def routed_block(key, own, number, rows, count, top, most, lean):
    sequence = jax.random.permutation(key, count)
    packed, common = load_shares(count, rows * top, most, lean, True), load_shares(count, rows * top, most, lean, False)
    places = jnp.arange(count)

    def named(lengths, turn):
        used = int((lengths > 0).sum())
        fixed = max(1, used // 4)
        passed = fixed + (places - fixed + turn * (used - fixed)) % max(1, count - fixed)
        return jnp.zeros((count,), jnp.int32).at[sequence[jnp.where(places < fixed, places, passed)]].set(jnp.asarray(lengths, jnp.int32))

    lengths = jnp.where(number % 4 == 0, named(packed, number // 4), named(common, number - number // 4 - 1))
    mixed = jax.random.permutation(jax.random.fold_in(own, 3), count)
    donor, sink = mixed[0:count // 2 * 2:2], mixed[1:count // 2 * 2:2]
    slack = jnp.minimum(lengths[donor] - 1, most - lengths[sink]) // 2
    slack = jnp.where((donor == sequence[0]) | (sink == sequence[0]) | (lengths[sink] == 0), 0, jnp.maximum(slack, 0))
    passed = jax.random.randint(jax.random.fold_in(own, 4), (count // 2,), 0, 1 << 20) % (slack + 1)
    lengths = lengths.at[donor].add(-passed).at[sink].add(passed)
    members = jnp.searchsorted(jnp.cumsum(lengths), jnp.arange(rows * top), side="right").astype(jnp.int32)
    grid = members.reshape(top, rows).T
    grid = grid[jax.random.permutation(jax.random.fold_in(own, 1), rows)]
    turn = jax.random.randint(jax.random.fold_in(own, 2), (rows, 1), 0, top)
    return jnp.take_along_axis(grid, (jnp.arange(top)[None, :] + turn) % top, axis=1)


def load_shares(number_of, total, most, slope, full):
    portions = [(1 << 20) // math.isqrt(rank ** slope) + 1 for rank in range(1, number_of + 1)]
    largest = most if full else min(most, max(-(-total // number_of), total * portions[0] // sum(portions)))
    least = 1 if total - largest >= number_of - 1 else 0
    holding, surplus = [largest] + [least] * (number_of - 1), total - largest - least * (number_of - 1)
    while surplus > 0:
        free = [i for i in range(1, number_of) if holding[i] < largest] or [i for i in range(1, number_of) if holding[i] < most]
        pool, left = sum([portions[i] for i in free]), surplus
        for i in free:
            extra = min(most - holding[i], max(1, left * portions[i] // pool), surplus)
            holding[i] = holding[i] + extra
            surplus = surplus - extra
    return np.array(holding)


def normal_values(rng, extent, width, most, split=(), held_as=jnp.bfloat16):
    entries = jax.random.normal(rng, extent, jnp.float32) * width
    if len(split) > 0:
        entries = block_levels(rng, extent, split, -0.22, 0.18) * entries
    return jnp.clip(entries, min=-most, max=most).astype(held_as)


def setup_inputs(seed: int = 0) -> dict:
    keys = jax.random.split(jax.random.key(seed), 10)
    queries = draw_queries(jax.random.fold_in(keys[9], 71), 0)
    rotated_key_heads = draw_rotated_key_heads(jax.random.fold_in(keys[9], 71), 0)
    stacked_value_heads = normal_values(keys[2], (SEQUENCE_LENGTH, KEY_VALUE_HEADS * HEAD_WIDTH), 1.0, 6.0, ((0, 32),))
    moe_rows = normal_values(keys[3], (MOE_TOKENS, D), 1.0, 6.0, ((0, 32),))
    expert_ids_keys = jax.random.split(jax.random.fold_in(keys[4], 1), MOE_TOKENS // MOE_TOK)
    expert_ids_turns = jax.random.permutation(jax.random.fold_in(keys[4], 3), MOE_TOKENS // MOE_TOK)
    expert_ids = jax.vmap(lambda own, number: routed_block(jax.random.fold_in(keys[4], 2), own, number, MOE_TOK, EXPERTS, TOPK, MOST, 1))(expert_ids_keys, expert_ids_turns).reshape((MOE_TOKENS, TOPK))
    route_weights = jnp.clip(0.05 + 0.29999999 * jax.random.uniform(keys[5], (MOE_TOKENS, TOPK), jnp.float32) ** block_levels(keys[5], (MOE_TOKENS, TOPK), ((0, 32),), -0.2, 0.2), 0.05, 0.35)
    w_gate = normal_values(keys[6], (EXPERTS, D, FFE), D ** -0.5, 0.09375, ((0, 32),))
    w_up = normal_values(keys[7], (EXPERTS, D, FFE), D ** -0.5, 0.09375, ((0, 32),))
    w_down = normal_values(keys[8], (EXPERTS, FFE, D), FFE ** -0.5, 0.21875, ((0, 32),))
    return dict(queries=queries, rotated_key_heads=rotated_key_heads, stacked_value_heads=stacked_value_heads, moe_rows=moe_rows, expert_ids=expert_ids, route_weights=route_weights, w_gate=w_gate, w_up=w_up, w_down=w_down)


def attention(queries, rotated_key_heads, stacked_value_heads):
    span_length = queries.shape[0]
    query_grid = queries.reshape(span_length, QUERY_HEADS, HEAD_WIDTH)
    key_lattice = rotated_key_heads.reshape(span_length, KEY_VALUE_HEADS, HEAD_WIDTH)
    value_lattice = stacked_value_heads.reshape(span_length, KEY_VALUE_HEADS, HEAD_WIDTH)
    group_width = QUERY_HEADS // KEY_VALUE_HEADS
    positions = jnp.arange(span_length, dtype=jnp.int32)
    causal = positions[None, :] <= positions[:, None]
    scale_factor = 1.0 / (HEAD_WIDTH ** 0.5)

    def one_head(head):
        query_head = lax.dynamic_index_in_dim(query_grid, head, 1, keepdims=False)
        key_head = lax.dynamic_index_in_dim(key_lattice, head // group_width, 1, keepdims=False)
        value_head = lax.dynamic_index_in_dim(value_lattice, head // group_width, 1, keepdims=False)
        scores = jnp.dot(query_head, key_head.T, preferred_element_type=jnp.float32) * scale_factor
        scores = jnp.where(causal, scores, -1e30)
        row_max = jnp.max(scores, axis=1, keepdims=True)
        probs = jnp.where(causal, jnp.exp(scores - row_max), 0.0).astype(jnp.bfloat16)
        denominator = jnp.sum(probs.astype(jnp.float32), axis=1)
        summed = jnp.dot(probs, value_head, preferred_element_type=jnp.float32)
        return (summed / denominator[:, None]).astype(jnp.bfloat16)

    heads_out = lax.map(one_head, jnp.arange(QUERY_HEADS, dtype=jnp.int32))
    return jnp.transpose(heads_out, (1, 0, 2)).reshape(span_length, QUERY_HEADS * HEAD_WIDTH)


def reference(queries, rotated_key_heads, stacked_value_heads, moe_rows, expert_ids, route_weights, w_gate, w_up, w_down):
    attended = attention(queries, rotated_key_heads, stacked_value_heads)
    total_rows = moe_rows.shape[0]
    pair_count = total_rows * TOPK
    flat_ids = expert_ids.reshape(pair_count)
    padded_rows = jnp.concatenate([moe_rows, jnp.zeros((1, D), moe_rows.dtype)], 0)
    padded_weights = jnp.concatenate([route_weights.reshape(pair_count), jnp.zeros((1,), route_weights.dtype)], 0)
    limit = MOST * N_CTX * N_EXP

    def add_expert(index, summed):
        selected = jnp.nonzero(flat_ids == index, size=limit, fill_value=pair_count)[0].astype(jnp.int32)
        token_index = selected // TOPK
        inputs = padded_rows[token_index]
        gate_in = jnp.dot(inputs, w_gate[index], preferred_element_type=jnp.float32)
        up_in = jnp.dot(inputs, w_up[index], preferred_element_type=jnp.float32)
        hidden = (jax.nn.silu(gate_in) * up_in).astype(jnp.bfloat16)
        output = jnp.dot(hidden, w_down[index], preferred_element_type=jnp.float32).astype(jnp.bfloat16)
        scaled = padded_weights[selected][:, None] * output.astype(jnp.float32)
        return summed.at[token_index].add(scaled)

    summed = lax.fori_loop(0, EXPERTS, add_expert, jnp.zeros((total_rows + 1, D), jnp.float32))
    return (attended, summed[:total_rows].astype(jnp.bfloat16))
```

```python
import functools
import math

import jax
import jax.numpy as jnp
from jax import lax
from jax.experimental import pallas as pl
from jax.experimental.pallas import tpu as pltpu
from jax.sharding import PartitionSpec as P

HEAD_WIDTH = 128
F32 = jnp.float32
BF16 = jnp.bfloat16


def swap(value, axis, offset):
    count = lax.axis_size(axis)
    return lax.ppermute(value, axis, [(i, i ^ offset) for i in range(count)])


def attention_kernel(heads, rows, q_ref, kv_ref, out_ref):
    here = lax.axis_index("ctx") * lax.axis_size("exp") + lax.axis_index("exp")
    first = here * rows
    query = jnp.concatenate(
        [q_ref[:, h * HEAD_WIDTH : (h + 1) * HEAD_WIDTH] for h in range(heads)], axis=0
    )
    scores = lax.dot_general(
        query, kv_ref[0], (((1,), (1,)), ((), ())), preferred_element_type=F32
    ) * (1.0 / math.sqrt(HEAD_WIDTH))
    place = lax.broadcasted_iota(jnp.int32, scores.shape, 1)
    position = place ^ first
    query_position = lax.broadcasted_iota(jnp.int32, scores.shape, 0) % rows + first
    allowed = position <= query_position
    scores = jnp.where(allowed, scores, -1e30)
    row_max = jnp.max(scores, axis=1, keepdims=True)
    probs = jnp.exp(scores - row_max).astype(BF16)
    total = jnp.sum(probs.astype(F32), axis=1, keepdims=True)
    summed = jnp.dot(probs, kv_ref[1], preferred_element_type=F32)
    result = (summed / total).astype(BF16)
    for h in range(heads):
        out_ref[:, h * HEAD_WIDTH : (h + 1) * HEAD_WIDTH] = result[h * rows : (h + 1) * rows]


def attend(queries, keys, values):
    rows, width = queries.shape
    kv_heads = keys.shape[1] // HEAD_WIDTH
    heads = width // HEAD_WIDTH // kv_heads
    ctx, exp = lax.axis_size("ctx"), lax.axis_size("exp")
    own = jnp.concatenate(
        [
            keys.reshape(rows, kv_heads, HEAD_WIDTH).transpose(1, 0, 2)[:, None],
            values.reshape(rows, kv_heads, HEAD_WIDTH).transpose(1, 0, 2)[:, None],
        ],
        axis=1,
    )
    line = jnp.concatenate([own] + [swap(own, "exp", s) for s in range(1, exp)], axis=2)
    group = [line] + [swap(line, "ctx", 2 * m) for m in range(1, ctx // 2)]
    mine = jnp.stack(group, axis=0)
    other = swap(mine, "ctx", 1)
    both = jnp.stack([mine, other], axis=1)
    gathered = both.transpose(2, 3, 0, 1, 4, 5).reshape(
        kv_heads, 2, ctx * exp * rows, HEAD_WIDTH
    )
    total_rows = ctx * exp * rows
    return pl.pallas_call(
        functools.partial(attention_kernel, heads, rows),
        grid=(kv_heads,),
        in_specs=[
            pl.BlockSpec((rows, heads * HEAD_WIDTH), lambda g: (0, g)),
            pl.BlockSpec((None, 2, total_rows, HEAD_WIDTH), lambda g: (g, 0, 0, 0)),
        ],
        out_specs=pl.BlockSpec((rows, heads * HEAD_WIDTH), lambda g: (0, g)),
        out_shape=jax.ShapeDtypeStruct(queries.shape, BF16),
        compiler_params=pltpu.CompilerParams(vmem_limit_bytes=48 * 1024 * 1024),
        cost_estimate=pl.CostEstimate(
            flops=4 * rows * width * total_rows,
            bytes_accessed=total_rows * kv_heads * 4 * HEAD_WIDTH + 4 * rows * width,
            transcendentals=rows * total_rows * heads * kv_heads,
        ),
    )(queries, gathered)


def mixture(moe_rows, expert_ids, route_weights, w_gate, w_up, w_down):
    ctx, exp = lax.axis_size("ctx"), lax.axis_size("exp")
    tokens, width = moe_rows.shape
    top = expert_ids.shape[1]
    experts = ctx * exp
    groups = ctx // 2
    capacity = max(2, tokens * top * 5 // (4 * experts))
    c, z = lax.axis_index("ctx"), lax.axis_index("exp")

    meta = jnp.concatenate([expert_ids.astype(F32).T, route_weights.T], axis=0)
    meta = jnp.concatenate([meta, swap(meta, "ctx", 1)], axis=1)
    metas = [meta] + [swap(meta, "exp", s) for s in range(1, exp)]
    own = [moe_rows] + [swap(moe_rows, "exp", s) for s in range(1, exp)]

    wanted = ((c ^ (2 * jnp.arange(groups))) * exp + z).astype(F32)
    earlier = jnp.arange(2 * tokens)
    before = (
        (earlier[:, None] < earlier[None, :])
        & (earlier[:, None] // tokens == earlier[None, :] // tokens)
    ).astype(BF16)

    def slots(meta):
        hit = meta[:top][None] == wanted[:, None, None]
        member = jnp.any(hit, axis=1)
        weight = jnp.sum(jnp.where(hit, meta[top:][None], 0.0), axis=1)
        rank = jnp.dot(member.astype(BF16), before, preferred_element_type=F32)
        block = earlier // tokens
        place = block[None, None, :, None, None]
        slot = jnp.arange(capacity, dtype=F32)
        taken = (
            member[:, None, None, :]
            & (rank[:, None, None, :] == slot[None, None, :, None])
            & (block[None, None, None, :] == jnp.arange(2)[None, :, None, None])
        )
        taken = taken.reshape(groups, 2 * capacity, 2 * tokens)
        return taken, weight

    def ffn(rows):
        gate = jnp.dot(rows, w_gate[0], preferred_element_type=F32)
        up = jnp.dot(rows, w_up[0], preferred_element_type=F32)
        hidden = (gate / (1.0 + jnp.exp(-gate)) * up).astype(BF16)
        return jnp.dot(hidden, w_down[0], preferred_element_type=F32).astype(BF16)

    partial = []
    for s in range(exp):
        taken, weight = slots(metas[s])
        block = jnp.concatenate([own[s], swap(own[s], "ctx", 1)], axis=0)
        sent = [
            jnp.dot(taken[m].astype(BF16), block, preferred_element_type=F32).astype(BF16)
            for m in range(groups)
        ]
        rows = jnp.concatenate(
            [sent[0]] + [swap(sent[m], "ctx", 2 * m) for m in range(1, groups)], axis=0
        )
        served = ffn(rows).reshape(groups, 2 * capacity, width)
        back = jnp.concatenate(
            [served[0]] + [swap(served[m], "ctx", 2 * m) for m in range(1, groups)], axis=0
        )
        scale = jnp.where(taken, weight[:, None, :], 0.0).reshape(
            groups * 2 * capacity, 2 * tokens
        )
        high = scale.astype(BF16)
        low = (scale - high.astype(F32)).astype(BF16)
        contract = (((0,), (0,)), ((), ()))
        mixed = lax.dot_general(high, back, contract, preferred_element_type=F32)
        mixed = mixed + lax.dot_general(low, back, contract, preferred_element_type=F32)
        total = mixed[:tokens] + swap(mixed[tokens:].astype(BF16), "ctx", 1).astype(F32)
        partial.append(total)
    summed = partial[0]
    for s in range(1, exp):
        summed = summed + swap(partial[s].astype(BF16), "exp", s).astype(F32)
    return summed.astype(BF16)


def body(queries, keys, values, moe_rows, expert_ids, route_weights, w_gate, w_up, w_down):
    attended = attend(queries, keys, values)
    expert_mix = mixture(moe_rows, expert_ids, route_weights, w_gate, w_up, w_down)
    return (attended, expert_mix)


def solution(mesh):
    row = P(("ctx", "exp"), None)
    cube = P(("ctx", "exp"), None, None)
    return jax.shard_map(
        body,
        mesh=mesh,
        in_specs=(row,) * 6 + (cube,) * 3,
        out_specs=(row, row),
        check_vma=False,
    )
```

```python
import functools
import math

import jax
import jax.numpy as jnp
from jax import lax
from jax.experimental import pallas as pl
from jax.experimental.pallas import tpu as pltpu
from jax.sharding import PartitionSpec as P

HEAD_WIDTH = 128
F32 = jnp.float32
BF16 = jnp.bfloat16
VMEM = 48 * 1024 * 1024
COSTS = {"pack1": 20, "pack2": 20, "pack3": 20, "ffn2": 15, "ffn3": 20}
COSTS.update({f"combine{s}": 40 for s in range(4)})


def cost(name):
    work = 1024 + int(COSTS.get(name, 0.0) * 1.0e9)
    return pl.CostEstimate(flops=work, bytes_accessed=1024, transcendentals=0)


PARAMS = pltpu.CompilerParams(vmem_limit_bytes=VMEM)
ANYWHERE = pl.BlockSpec(memory_space=pl.ANY)


def swap(value, axis, offset):
    count = lax.axis_size(axis)
    return lax.ppermute(value, axis, [(i, i ^ offset) for i in range(count)])


def exchange(value):
    return lax.all_to_all(value, "ctx", split_axis=0, concat_axis=0, tiled=True)


def gate(name, value, after):
    return pl.pallas_call(
        lambda value_ref, after_ref, out_ref: None,
        in_specs=[ANYWHERE, ANYWHERE],
        out_specs=ANYWHERE,
        out_shape=jax.ShapeDtypeStruct(value.shape, value.dtype),
        input_output_aliases={0: 0},
        cost_estimate=cost(name),
    )(value, after)


def attention_kernel(heads, blocks, rows, q_ref, kv_ref, after_ref, arrived_ref, out_ref):
    exp = lax.axis_size("exp")
    ctx = lax.axis_size("ctx")
    z = lax.axis_index("exp")
    q = q_ref[...].reshape(blocks * rows, heads * HEAD_WIDTH)
    query = jnp.concatenate(
        [q[:, h * HEAD_WIDTH : (h + 1) * HEAD_WIDTH] for h in range(heads)], axis=0
    )
    scores = lax.dot_general(
        query, kv_ref[:, :HEAD_WIDTH], (((1,), (1,)), ((), ())), preferred_element_type=F32
    ) * (1.0 / math.sqrt(HEAD_WIDTH))
    shape = (1, scores.shape[1])
    place = lax.broadcasted_iota(jnp.int32, shape, 1)
    block = place // rows
    position = ((block % ctx) * exp + ((block // ctx) ^ z)) * rows + place % rows
    shape = (scores.shape[0], 1)
    row = lax.broadcasted_iota(jnp.int32, shape, 0) % (blocks * rows)
    query_block = pl.program_id(0) * blocks + row // rows
    query_position = (query_block * exp + z) * rows + row % rows
    scores = jnp.where(position <= query_position, scores, -1e30)
    row_max = jnp.max(scores, axis=1, keepdims=True)
    probs = jnp.exp(scores - row_max).astype(BF16)
    total = jnp.sum(probs.astype(F32), axis=1, keepdims=True)
    summed = jnp.dot(probs, kv_ref[:, HEAD_WIDTH:], preferred_element_type=F32)
    result = (summed / total).astype(BF16)
    here = blocks * rows
    out_ref[...] = jnp.concatenate(
        [result[h * here : (h + 1) * here] for h in range(heads)], axis=1
    ).reshape(out_ref.shape)


def attend(queries, line, after, arrived):
    ctx, rows, width = queries.shape
    blocks = max(1, ctx // 4)
    return pl.pallas_call(
        functools.partial(attention_kernel, width // HEAD_WIDTH, blocks, rows),
        grid=(ctx // blocks,),
        in_specs=[
            pl.BlockSpec((blocks, rows, width), lambda g: (g, 0, 0)),
            pl.BlockSpec(line.shape, lambda g: (0, 0)),
            ANYWHERE,
            ANYWHERE,
        ],
        out_specs=pl.BlockSpec((blocks, rows, width), lambda g: (g, 0, 0)),
        out_shape=jax.ShapeDtypeStruct(queries.shape, BF16),
        compiler_params=PARAMS,
        cost_estimate=cost("attend"),
    )(queries, line, after, arrived)


def slot_matrix(meta_ref, plan, weighted):
    places, capacity, top, rows = plan
    tokens = meta_ref.shape[1]
    z, exp = lax.axis_index("exp"), lax.axis_size("exp")
    ids = meta_ref[:top]
    weights = meta_ref[top:]
    members, scales = [], []
    for m in range(places):
        hit = ids == (m * exp + z).astype(F32)
        members.append(jnp.sum(jnp.where(hit, 1.0, 0.0), axis=0, keepdims=True))
        scales.append(jnp.sum(jnp.where(hit, weights, 0.0), axis=0, keepdims=True))
    member = jnp.concatenate(members, axis=0)
    first = lax.broadcasted_iota(jnp.int32, (tokens, tokens), 0)
    second = lax.broadcasted_iota(jnp.int32, (tokens, tokens), 1)
    before = jnp.where(first < second, 1.0, 0.0).astype(BF16)
    rank = jnp.dot(member.astype(BF16), before, preferred_element_type=F32)
    rank = jnp.where(member > 0.5, rank, -1.0).astype(jnp.int32)
    slot = lax.broadcasted_iota(jnp.int32, (rows, tokens), 0)
    return jnp.concatenate(
        [
            jnp.where(slot == rank[m : m + 1], scales[m] if weighted else 1.0, 0.0)
            for m in range(places)
        ],
        axis=0,
    )


def pack_kernel(plan, copies, meta_ref, after_ref, arrived_ref, *refs):
    halves, refs = refs[:2], refs[2:]
    if copies:
        refs[3][...] = refs[0][...]
        refs[4][...] = refs[1][...]
        refs = (refs[2], refs[-1])
    out_ref, pick_ref = refs

    @pl.when(pl.program_id(0) == 0)
    def _():
        pick_ref[...] = slot_matrix(meta_ref, plan, False).astype(BF16)

    block = jnp.concatenate([ref[...] for ref in halves], axis=0)
    out_ref[...] = jnp.dot(pick_ref[...], block, preferred_element_type=F32).astype(BF16)


def pack(stage, meta, halves, after, arrived, extra, plan):
    places, capacity, top, rows = plan
    half, width = halves[0].shape
    columns = width // 4
    tile = pl.BlockSpec((half, columns), lambda i: (0, i))
    operands = [meta, after, arrived, *halves]
    in_specs = [pl.BlockSpec(meta.shape, lambda i: (0, 0)), ANYWHERE, ANYWHERE, tile, tile]
    out_specs = [pl.BlockSpec((places * rows, columns), lambda i: (0, i))]
    out_shape = [jax.ShapeDtypeStruct((places * rows, width), BF16)]
    if extra is not None:
        operands += extra
        in_specs += [tile, tile]
        out_specs += [tile, tile]
        out_shape += [jax.ShapeDtypeStruct((half, width), BF16)] * 2
    return pl.pallas_call(
        functools.partial(pack_kernel, plan, extra is not None),
        grid=(width // columns,),
        in_specs=in_specs,
        out_specs=out_specs,
        out_shape=out_shape,
        scratch_shapes=[pltpu.VMEM((places * rows, 2 * half), BF16)],
        compiler_params=PARAMS,
        cost_estimate=cost(f"pack{stage}"),
    )(*operands)


def ffn_kernel(x_ref, gate_ref, up_ref, down_ref, after_ref, out_ref, total_ref):
    step, last = pl.program_id(0), pl.num_programs(0) - 1
    x = x_ref[...]
    gated = jnp.dot(x, gate_ref[0], preferred_element_type=F32)
    up = jnp.dot(x, up_ref[0], preferred_element_type=F32)
    hidden = (gated / (1.0 + jnp.exp(-gated)) * up).astype(BF16)
    term = jnp.dot(hidden, down_ref[0], preferred_element_type=F32)

    @pl.when(step == 0)
    def _():
        total_ref[...] = term

    @pl.when((step > 0) & (step < last))
    def _():
        total_ref[...] += term

    @pl.when(step == last)
    def _():
        out_ref[...] = (total_ref[...] + term).astype(BF16)


def ffn(stage, x, w_gate, w_up, w_down, after):
    rows, width = x.shape
    hidden = w_gate.shape[2]
    block = 256
    whole = pl.BlockSpec((rows, width), lambda i: (0, 0))
    return pl.pallas_call(
        ffn_kernel,
        grid=(hidden // block,),
        in_specs=[
            whole,
            pl.BlockSpec((1, width, block), lambda i: (0, 0, i)),
            pl.BlockSpec((1, width, block), lambda i: (0, 0, i)),
            pl.BlockSpec((1, block, width), lambda i: (0, i, 0)),
            ANYWHERE,
        ],
        out_specs=whole,
        out_shape=jax.ShapeDtypeStruct((rows, width), BF16),
        scratch_shapes=[pltpu.VMEM((rows, width), F32)],
        compiler_params=PARAMS,
        cost_estimate=cost(f"ffn{stage}"),
    )(x, w_gate, w_up, w_down, after)


def combine_kernel(plan, meta_ref, back_ref, after_ref, *refs):
    outs, (high_ref, low_ref) = refs[:-2], refs[-2:]

    @pl.when(pl.program_id(0) == 0)
    def _():
        scale = slot_matrix(meta_ref, plan, True)
        high = scale.astype(BF16)
        high_ref[...] = high
        low_ref[...] = (scale - high.astype(F32)).astype(BF16)

    back = back_ref[...]
    contract = (((0,), (0,)), ((), ()))
    mixed = lax.dot_general(high_ref[...], back, contract, preferred_element_type=F32)
    mixed = mixed + lax.dot_general(low_ref[...], back, contract, preferred_element_type=F32)
    rows = outs[0].shape[0]
    for index, ref in enumerate(outs):
        ref[...] = mixed[index * rows : (index + 1) * rows].astype(ref.dtype)


def combine(stage, meta, back, after, outs, dtype, plan):
    tokens = meta.shape[1]
    slots, width = back.shape
    columns = width // 4
    return pl.pallas_call(
        functools.partial(combine_kernel, plan),
        grid=(width // columns,),
        in_specs=[
            pl.BlockSpec(meta.shape, lambda i: (0, 0)),
            pl.BlockSpec((slots, columns), lambda i: (0, i)),
            ANYWHERE,
        ],
        out_specs=[pl.BlockSpec((tokens // outs, columns), lambda i: (0, i))] * outs,
        out_shape=[jax.ShapeDtypeStruct((tokens // outs, width), dtype)] * outs,
        scratch_shapes=[pltpu.VMEM((slots, tokens), BF16)] * 2,
        compiler_params=PARAMS,
        cost_estimate=cost(f"combine{stage}"),
    )(meta, back, after)


def finish_kernel(pieces, own_ref, *refs):
    out_ref = refs[-1]
    parts = [jnp.concatenate([refs[i][...] for i in group], axis=0) for group in pieces]
    total = own_ref[...]
    for part in parts:
        total = total + part.astype(F32)
    out_ref[...] = total.astype(BF16)


def finish(own, parts):
    tokens, width = own.shape
    columns = width // 4
    tile = pl.BlockSpec((tokens, columns), lambda i: (0, i))
    flat = [piece for part in parts for piece in part]
    pieces, start = [], 0
    for part in parts:
        pieces.append(range(start, start + len(part)))
        start += len(part)
    return pl.pallas_call(
        functools.partial(finish_kernel, pieces),
        grid=(width // columns,),
        in_specs=[tile]
        + [pl.BlockSpec((piece.shape[0], columns), lambda i: (0, i)) for piece in flat],
        out_specs=tile,
        out_shape=jax.ShapeDtypeStruct(own.shape, BF16),
        compiler_params=PARAMS,
        cost_estimate=cost("finish"),
    )(own, *flat)


def body(queries, keys, values, moe_rows, expert_ids, route_weights, w_gate, w_up, w_down):
    ctx, exp = lax.axis_size("ctx"), lax.axis_size("exp")
    sequence, query_width = queries.shape
    kv_heads = keys.shape[1] // HEAD_WIDTH
    tokens, width = moe_rows.shape
    top = expert_ids.shape[1]
    capacity = max(2, tokens * top * 5 // (4 * ctx * exp))
    rows = -(-capacity // 8) * 8
    plan = (ctx, capacity, top, rows)

    meta = jnp.concatenate([expert_ids.astype(F32).T, route_weights.T], axis=0)
    metas = [meta] + [swap(meta, "exp", s) for s in range(1, exp)]
    mine = [moe_rows[: tokens // 2], moe_rows[tokens // 2 :]]

    q = queries.reshape(sequence, ctx, query_width // ctx).transpose(1, 0, 2)
    k = keys.reshape(sequence, kv_heads, HEAD_WIDTH).transpose(1, 0, 2)
    v = values.reshape(sequence, kv_heads, HEAD_WIDTH).transpose(1, 0, 2)
    kv = jnp.repeat(jnp.concatenate([k, v], axis=2), ctx // kv_heads, axis=0)
    heads = exchange(jnp.concatenate([q, kv], axis=2))
    local_queries = heads[:, :, : query_width // ctx]
    local_kv = heads[:, :, query_width // ctx :].reshape(ctx * sequence, 2 * HEAD_WIDTH)

    sent, served, partial, arrived = {}, {}, {}, {0: mine}
    state = {"after": queries, "held": mine}

    def dispatch(s):
        if s > 0:
            source = state["held"] if s > 2 else mine
            arrived[s] = [swap(part, "exp", s) for part in source]
        earlier = sent[s - 2] if s > 1 else heads if s == 1 else queries
        result = pack(
            s, metas[s], arrived[s], state["after"], earlier, mine if s == 1 else None, plan
        )
        if s == 1:
            state["held"] = result[1:]
        sent[s] = exchange(result[0].reshape(ctx, rows, width))
        state["after"] = result[0]

    def serve(s):
        x = sent[s].reshape(ctx * rows, width)
        served[s] = ffn(s, x, w_gate, w_up, w_down, state["after"])
        state["after"] = served[s]

    def give_back(s, arrived):
        out = served[s] if arrived is None else gate(f"back{s}", served[s], arrived)
        served[s] = exchange(out.reshape(ctx, rows, width))

    def collect(s):
        back = served[s].reshape(ctx * rows, width)
        if s == 0:
            partial[s] = combine(s, metas[s], back, state["after"], 1, F32, plan)
        else:
            outs = combine(s, metas[s], back, state["after"], 1 if s == 1 else 2, BF16, plan)
            partial[s] = [swap(out, "exp", s) for out in outs]
            state["after"] = outs[0]

    dispatch(0)
    dispatch(1)
    serve(0)
    dispatch(2)
    serve(1)
    for s in range(3, exp):
        dispatch(s)
    held_kv = gate("kv", local_kv, state["after"])
    state["after"] = held_kv
    line = jnp.concatenate([held_kv] + [swap(held_kv, "exp", s) for s in range(1, exp)], axis=0)
    serve(2)
    attended = attend(local_queries, line, state["after"], sent[exp - 1])
    state["after"] = attended
    for s in range(3, exp):
        serve(s)
    order = list(range(2, exp)) + [1, 0]
    arrived_back = None
    for s in order:
        give_back(s, arrived_back)
        arrived_back = served[s]
    output = exchange(gate("out", attended, arrived_back))
    for s in order:
        collect(s)
    mixed = finish(partial[0][0], [partial[s] for s in range(1, exp)])
    return (output.transpose(1, 0, 2).reshape(sequence, query_width), mixed)


def solution(mesh):
    row = P(("ctx", "exp"), None)
    cube = P(("ctx", "exp"), None, None)
    return jax.shard_map(
        body,
        mesh=mesh,
        in_specs=(row,) * 6 + (cube,) * 3,
        out_specs=(row, row),
        check_vma=False,
    )
```

```python
import functools
import math

import jax
import jax.numpy as jnp
from jax import lax
from jax.experimental import pallas as pl
from jax.experimental.pallas import tpu as pltpu
from jax.sharding import PartitionSpec as P

HEAD_WIDTH = 128
F32 = jnp.float32
BF16 = jnp.bfloat16
VMEM = 48 * 1024 * 1024
COSTS = {"pack1": 20, "pack2": 20, "pack3": 20, "ffn2": 15, "ffn3": 20, "heads": 20}
COSTS.update({f"combine{s}": 40 for s in range(4)})


def cost(name):
    work = 1024 + int(COSTS.get(name, 0.0) * 1.0e9)
    return pl.CostEstimate(flops=work, bytes_accessed=1024, transcendentals=0)


PARAMS = pltpu.CompilerParams(vmem_limit_bytes=VMEM)
ANYWHERE = pl.BlockSpec(memory_space=pl.ANY)
TOKEN = pl.BlockSpec((8, 128), lambda *step: (0, 0))
TOKEN_SHAPE = jax.ShapeDtypeStruct((8, 128), F32)


def swap(value, axis, offset):
    count = lax.axis_size(axis)
    return lax.ppermute(value, axis, [(i, i ^ offset) for i in range(count)])


def exchange(value):
    return lax.all_to_all(value, "ctx", split_axis=0, concat_axis=0, tiled=True)


def gate(name, values, after):
    return pl.pallas_call(
        lambda *refs: None,
        in_specs=[ANYWHERE] * (len(values) + 1),
        out_specs=[ANYWHERE] * len(values),
        out_shape=[jax.ShapeDtypeStruct(value.shape, value.dtype) for value in values],
        input_output_aliases={i: i for i in range(len(values))},
        cost_estimate=cost(name),
    )(*values, after)


def attention_kernel(heads, blocks, rows, q_ref, kv_ref, after_ref, out_ref, token_ref):
    token_ref[...] = jnp.zeros(token_ref.shape, F32)
    exp = lax.axis_size("exp")
    ctx = lax.axis_size("ctx")
    z = lax.axis_index("exp")
    q = q_ref[...].reshape(blocks * rows, heads * HEAD_WIDTH)
    query = jnp.concatenate(
        [q[:, h * HEAD_WIDTH : (h + 1) * HEAD_WIDTH] for h in range(heads)], axis=0
    )
    scores = lax.dot_general(
        query, kv_ref[:, :HEAD_WIDTH], (((1,), (1,)), ((), ())), preferred_element_type=F32
    ) * (1.0 / math.sqrt(HEAD_WIDTH))
    shape = (1, scores.shape[1])
    place = lax.broadcasted_iota(jnp.int32, shape, 1)
    block = place // rows
    position = ((block % ctx) * exp + ((block // ctx) ^ z)) * rows + place % rows
    shape = (scores.shape[0], 1)
    row = lax.broadcasted_iota(jnp.int32, shape, 0) % (blocks * rows)
    query_block = pl.program_id(0) * blocks + row // rows
    query_position = (query_block * exp + z) * rows + row % rows
    scores = jnp.where(position <= query_position, scores, -1e30)
    row_max = jnp.max(scores, axis=1, keepdims=True)
    probs = jnp.exp(scores - row_max).astype(BF16)
    total = jnp.sum(probs.astype(F32), axis=1, keepdims=True)
    summed = jnp.dot(probs, kv_ref[:, HEAD_WIDTH:], preferred_element_type=F32)
    result = (summed / total).astype(BF16)
    here = blocks * rows
    out_ref[...] = jnp.concatenate(
        [result[h * here : (h + 1) * here] for h in range(heads)], axis=1
    ).reshape(out_ref.shape)


def attend(queries, line, after):
    ctx, rows, width = queries.shape
    blocks = max(1, ctx // 4)
    return pl.pallas_call(
        functools.partial(attention_kernel, width // HEAD_WIDTH, blocks, rows),
        grid=(ctx // blocks,),
        in_specs=[
            pl.BlockSpec((blocks, rows, width), lambda g: (g, 0, 0)),
            pl.BlockSpec(line.shape, lambda g: (0, 0)),
            ANYWHERE,
        ],
        out_specs=[pl.BlockSpec((blocks, rows, width), lambda g: (g, 0, 0)), TOKEN],
        out_shape=[jax.ShapeDtypeStruct(queries.shape, BF16), TOKEN_SHAPE],
        compiler_params=PARAMS,
        cost_estimate=cost("attend"),
    )(queries, line, after)


def slot_matrix(meta_ref, plan, weighted, relative=False):
    places, capacity, top, rows = plan
    tokens = meta_ref.shape[1]
    z, exp = lax.axis_index("exp"), lax.axis_size("exp")
    ids = meta_ref[:top]
    weights = meta_ref[top:]
    members, scales = [], []
    here = lax.axis_index("ctx") if relative else 0
    for m in range(places):
        hit = ids == ((here ^ m) * exp + z).astype(F32)
        members.append(jnp.sum(jnp.where(hit, 1.0, 0.0), axis=0, keepdims=True))
        scales.append(jnp.sum(jnp.where(hit, weights, 0.0), axis=0, keepdims=True))
    member = jnp.concatenate(members, axis=0)
    first = lax.broadcasted_iota(jnp.int32, (tokens, tokens), 0)
    second = lax.broadcasted_iota(jnp.int32, (tokens, tokens), 1)
    before = jnp.where(first < second, 1.0, 0.0).astype(BF16)
    rank = jnp.dot(member.astype(BF16), before, preferred_element_type=F32)
    rank = jnp.where(member > 0.5, rank, -1.0).astype(jnp.int32)
    slot = lax.broadcasted_iota(jnp.int32, (rows, tokens), 0)
    return jnp.concatenate(
        [
            jnp.where(slot == rank[m : m + 1], scales[m] if weighted else 1.0, 0.0)
            for m in range(places)
        ],
        axis=0,
    )


def pack_kernel(plan, count, other, meta_ref, after_ref, arrived_ref, *refs):
    pieces, refs = refs[:count], refs[count:]
    block = jnp.concatenate([ref[...] for ref in pieces], axis=0)
    held = block
    if other:
        held, refs = refs[0][...], refs[1:]
    out_ref, token_ref, *copies, pick_ref = refs
    token_ref[...] = jnp.zeros(token_ref.shape, F32)

    @pl.when(pl.program_id(0) == 0)
    def _():
        pick_ref[...] = slot_matrix(meta_ref, plan, False).astype(BF16)

    out_ref[...] = jnp.dot(pick_ref[...], block, preferred_element_type=F32).astype(BF16)
    start = 0
    for ref in copies:
        ref[...] = held[start % held.shape[0] :][: ref.shape[0]]
        start += ref.shape[0]


def pack(stage, meta, pieces, after, arrived, other, cuts, plan):
    places, capacity, top, rows = plan
    tokens, width = meta.shape[1], pieces[0].shape[1]
    columns = width // 4

    def tile(size):
        return pl.BlockSpec((size, columns), lambda i: (0, i))

    operands = [meta, after, arrived, *pieces]
    in_specs = [pl.BlockSpec(meta.shape, lambda i: (0, 0)), ANYWHERE, ANYWHERE]
    in_specs += [tile(piece.shape[0]) for piece in pieces]
    if other is not None:
        operands.append(other)
        in_specs.append(tile(tokens))
    out_specs = [tile(places * rows), TOKEN] + [tile(size) for size in cuts]
    out_shape = [jax.ShapeDtypeStruct((places * rows, width), BF16), TOKEN_SHAPE]
    out_shape += [jax.ShapeDtypeStruct((size, width), BF16) for size in cuts]
    return pl.pallas_call(
        functools.partial(pack_kernel, plan, len(pieces), other is not None),
        grid=(width // columns,),
        in_specs=in_specs,
        out_specs=out_specs,
        out_shape=out_shape,
        scratch_shapes=[pltpu.VMEM((places * rows, tokens), BF16)],
        compiler_params=PARAMS,
        cost_estimate=cost(f"pack{stage}"),
    )(*operands)


def ffn_kernel(split, x_ref, gate_ref, up_ref, down_ref, after_ref, *refs):
    *outs, token_ref, total_ref = refs
    token_ref[...] = jnp.zeros(token_ref.shape, F32)
    step, last = pl.program_id(0), pl.num_programs(0) - 1
    x = x_ref[...]
    gated = jnp.dot(x, gate_ref[0], preferred_element_type=F32)
    up = jnp.dot(x, up_ref[0], preferred_element_type=F32)
    hidden = (gated / (1.0 + jnp.exp(-gated)) * up).astype(BF16)
    term = jnp.dot(hidden, down_ref[0], preferred_element_type=F32)

    @pl.when(step == 0)
    def _():
        total_ref[...] = term

    @pl.when((step > 0) & (step < last))
    def _():
        total_ref[...] += term

    @pl.when(step == last)
    def _():
        if not split:
            outs[0][...] = (total_ref[...] + term).astype(BF16)
        else:
            total_ref[...] += term
            rows = outs[0].shape[0]
            for m, out_ref in enumerate(outs):
                start = pl.multiple_of((lax.axis_index("ctx") ^ m) * rows, 8)
                out_ref[...] = total_ref[pl.ds(start, rows)].astype(BF16)


def ffn(stage, x, w_gate, w_up, w_down, after, split):
    rows, width = x.shape
    hidden = w_gate.shape[2]
    block = 256
    whole = pl.BlockSpec((rows, width), lambda i: (0, 0))
    part = pl.BlockSpec((rows // split, width), lambda i: (0, 0))
    return pl.pallas_call(
        functools.partial(ffn_kernel, split > 1),
        grid=(hidden // block,),
        in_specs=[
            whole,
            pl.BlockSpec((1, width, block), lambda i: (0, 0, i)),
            pl.BlockSpec((1, width, block), lambda i: (0, 0, i)),
            pl.BlockSpec((1, block, width), lambda i: (0, i, 0)),
            ANYWHERE,
        ],
        out_specs=[part] * split + [TOKEN],
        out_shape=[jax.ShapeDtypeStruct((rows // split, width), BF16)] * split + [TOKEN_SHAPE],
        scratch_shapes=[pltpu.VMEM((rows, width), F32)],
        compiler_params=PARAMS,
        cost_estimate=cost(f"ffn{stage}"),
    )(x, w_gate, w_up, w_down, after)


def combine_kernel(plan, backs, count, meta_ref, after_ref, *refs):
    back_refs, pieces, refs = refs[:backs], refs[backs : backs + count], refs[backs + count :]
    outs, (token_ref, high_ref, low_ref) = refs[:-3], refs[-3:]
    token_ref[...] = jnp.zeros(token_ref.shape, F32)

    @pl.when(pl.program_id(0) == 0)
    def _():
        scale = slot_matrix(meta_ref, plan, True, backs > 1)
        high = scale.astype(BF16)
        high_ref[...] = high
        low_ref[...] = (scale - high.astype(F32)).astype(BF16)

    back = back_refs[0][...]
    if backs > 1:
        parts = [ref[...].astype(F32) for ref in back_refs]
        back = jnp.concatenate(parts, axis=0).astype(BF16)
    contract = (((0,), (0,)), ((), ()))
    mixed = lax.dot_general(high_ref[...], back, contract, preferred_element_type=F32)
    mixed = mixed + lax.dot_general(low_ref[...], back, contract, preferred_element_type=F32)
    if count:
        mixed = mixed + jnp.concatenate([ref[...] for ref in pieces], axis=0).astype(F32)
    rows = outs[0].shape[0]
    for index, ref in enumerate(outs):
        ref[...] = mixed[index * rows : (index + 1) * rows].astype(ref.dtype)


def combine(stage, meta, backs, after, pieces, outs, dtype, plan):
    tokens = meta.shape[1]
    width = backs[0].shape[1]
    slots = plan[0] * plan[3]
    columns = width // 4

    def tile(size):
        return pl.BlockSpec((size, columns), lambda i: (0, i))

    return pl.pallas_call(
        functools.partial(combine_kernel, plan, len(backs), len(pieces)),
        grid=(width // columns,),
        in_specs=[pl.BlockSpec(meta.shape, lambda i: (0, 0)), ANYWHERE]
        + [tile(piece.shape[0]) for piece in [*backs, *pieces]],
        out_specs=[tile(tokens // outs)] * outs + [TOKEN],
        out_shape=[jax.ShapeDtypeStruct((tokens // outs, width), dtype)] * outs + [TOKEN_SHAPE],
        scratch_shapes=[pltpu.VMEM((slots, tokens), BF16)] * 2,
        compiler_params=PARAMS,
        cost_estimate=cost(f"combine{stage}"),
    )(meta, after, *backs, *pieces)


def finish_kernel(pieces, own_ref, *refs):
    out_ref = refs[-1]
    parts = [jnp.concatenate([refs[i][...] for i in group], axis=0) for group in pieces]
    total = own_ref[...]
    for part in parts:
        total = total + part.astype(F32)
    out_ref[...] = total.astype(BF16)


def finish(own, parts):
    tokens, width = own.shape
    columns = width // 4
    tile = pl.BlockSpec((tokens, columns), lambda i: (0, i))
    flat = [piece for part in parts for piece in part]
    pieces, start = [], 0
    for part in parts:
        pieces.append(range(start, start + len(part)))
        start += len(part)
    return pl.pallas_call(
        functools.partial(finish_kernel, pieces),
        grid=(width // columns,),
        in_specs=[tile]
        + [pl.BlockSpec((piece.shape[0], columns), lambda i: (0, i)) for piece in flat],
        out_specs=tile,
        out_shape=jax.ShapeDtypeStruct(own.shape, BF16),
        compiler_params=PARAMS,
        cost_estimate=cost("finish"),
    )(own, *flat)


def body(queries, keys, values, moe_rows, expert_ids, route_weights, w_gate, w_up, w_down):
    ctx, exp = lax.axis_size("ctx"), lax.axis_size("exp")
    sequence, query_width = queries.shape
    kv_heads = keys.shape[1] // HEAD_WIDTH
    tokens, width = moe_rows.shape
    top = expert_ids.shape[1]
    capacity = max(2, tokens * top * 5 // (4 * ctx * exp))
    rows = -(-capacity // 8) * 8
    plan = (ctx, capacity, top, rows)

    meta = jnp.concatenate([expert_ids.astype(F32).T, route_weights.T], axis=0)
    metas = [meta] + [swap(meta, "exp", s) for s in range(1, exp)]
    state = {"after": sum(metas[1:])[:8]}
    sent, served, partial, arrived = {}, {}, {}, {0: [moe_rows]}

    def mark(value):
        return value.reshape(-1, value.shape[-1])[:8, :128].astype(F32)

    q = queries.reshape(sequence, ctx, query_width // ctx).transpose(1, 0, 2)
    k = keys.reshape(sequence, kv_heads, HEAD_WIDTH).transpose(1, 0, 2)
    v = values.reshape(sequence, kv_heads, HEAD_WIDTH).transpose(1, 0, 2)
    kv = jnp.repeat(jnp.concatenate([k, v], axis=2), ctx // kv_heads, axis=0)
    (heads,) = gate("heads", [jnp.concatenate([q, kv], axis=2)], state["after"])
    heads = exchange(heads)
    local_queries = heads[:, :, : query_width // ctx]
    local_kv = heads[:, :, query_width // ctx :].reshape(ctx * sequence, 2 * HEAD_WIDTH)

    halves = [tokens // 2] * 2
    mine = [moe_rows[: tokens // 2], moe_rows[tokens // 2 :]]
    for s in range(1, min(exp, 3)):
        arrived[s] = [swap(piece, "exp", s) for piece in mine]

    def dispatch(s, after):
        other, cuts = (moe_rows, halves) if s == 1 else (None, [])
        result = pack(s, metas[s], arrived[s], state["after"], after, other, cuts, plan)
        if s == 1:
            for t in range(3, exp):
                arrived[t] = [swap(piece, "exp", t) for piece in result[2:]]
        sent[s] = exchange(result[0].reshape(ctx, rows, width))
        state["after"] = result[1]

    def serve(s):
        x = sent[s].reshape(ctx * rows, width)
        split = ctx if s == 1 else 1
        *outs, state["after"] = ffn(s, x, w_gate, w_up, w_down, state["after"], split)
        served[s] = outs[0]
        if s == 1:
            served[s] = outs

    def pass_on(name, group, after):
        values = [served[1][m] for m in group]
        if after is not None:
            values = gate(name, values, after)
        for m, value in zip(group, values):
            served[1][m] = swap(value, "ctx", m)

    def passed(group):
        state["after"] = state["after"] + sum(mark(served[1][m]) for m in group)

    def give_back(s, before):
        out = served[s] if before is None else gate(f"back{s}", [served[s]], before)[0]
        served[s] = exchange(out.reshape(ctx, rows, width))

    def collect(s):
        backs = served[s] if s == 1 else [served[s].reshape(ctx * rows, width)]
        outs, dtype = (1, F32) if s == 0 else (1, BF16) if s == 1 else (2, BF16)
        pieces = partial[2] if s == 0 else []
        *parts, state["after"] = combine(
            s, metas[s], backs, state["after"], pieces, outs, dtype, plan
        )
        partial[s] = parts if s == 0 else [swap(part, "exp", s) for part in parts]

    third = max(1, ctx // 4)
    groups = [range(1, 1 + third), range(1 + third, 1 + 2 * third), range(1 + 2 * third, ctx)]
    dispatch(0, state["after"])
    dispatch(1, mark(heads))
    serve(0)
    dispatch(2, state["after"])
    serve(1)
    pass_on("pass0", groups[0], None)
    for s in range(3, exp):
        dispatch(s, state["after"])
    (held_kv,) = gate("kv", [local_kv], state["after"])
    line = jnp.concatenate([held_kv] + [swap(held_kv, "exp", s) for s in range(1, exp)], axis=0)
    state["after"] = mark(held_kv)
    serve(2)
    pass_on("pass1", groups[1], state["after"])
    passed(groups[0])
    order = list(range(2, exp)) + [0]
    give_back(2, None)
    attended, state["after"] = attend(local_queries, line, state["after"])
    passed(groups[1])
    pass_on("pass2", groups[2], state["after"])
    for s in range(3, exp):
        serve(s)
    for s in range(3, exp):
        give_back(s, mark(served[s - 1]))
    collect(2)
    give_back(0, mark(served[exp - 1]))
    collect(1)
    for s in range(3, exp):
        collect(s)
    collect(0)
    (attended,) = gate("out", [attended], mark(served[0]))
    output = exchange(attended).transpose(1, 0, 2).reshape(sequence, query_width)
    return (output, finish(partial[0][0], [partial[s] for s in [1, *range(3, exp)]]))


def solution(mesh):
    row = P(("ctx", "exp"), None)
    cube = P(("ctx", "exp"), None, None)
    return jax.shard_map(
        body,
        mesh=mesh,
        in_specs=(row,) * 6 + (cube,) * 3,
        out_specs=(row, row),
        check_vma=False,
    )
```

```python
import functools
import math

import jax
import jax.numpy as jnp
from jax import lax
from jax.experimental import pallas as pl
from jax.experimental.pallas import tpu as pltpu
from jax.sharding import PartitionSpec as P

HEAD_WIDTH = 128
F32 = jnp.float32
BF16 = jnp.bfloat16
VMEM = 48 * 1024 * 1024
COSTS = {"pack1": 20, "pack2": 40, "pack3": 20, "ffn2": 15, "ffn3": 20}
COSTS.update({f"combine{s}": 40 for s in range(4)})


def cost(name):
    work = 1024 + int(COSTS.get(name, 0.0) * 1.0e9)
    return pl.CostEstimate(flops=work, bytes_accessed=1024, transcendentals=0)


PARAMS = pltpu.CompilerParams(vmem_limit_bytes=VMEM)
ANYWHERE = pl.BlockSpec(memory_space=pl.ANY)
TOKEN = pl.BlockSpec((8, 128), lambda *step: (0, 0))
TOKEN_SHAPE = jax.ShapeDtypeStruct((8, 128), F32)


def swap(value, axis, offset):
    count = lax.axis_size(axis)
    return lax.ppermute(value, axis, [(i, i ^ offset) for i in range(count)])


def exchange(value):
    return lax.all_to_all(value, "ctx", split_axis=0, concat_axis=0, tiled=True)


def gate(name, values, after):
    return pl.pallas_call(
        lambda *refs: None,
        in_specs=[ANYWHERE] * (len(values) + 1),
        out_specs=[ANYWHERE] * len(values),
        out_shape=[jax.ShapeDtypeStruct(value.shape, value.dtype) for value in values],
        input_output_aliases={i: i for i in range(len(values))},
        cost_estimate=cost(name),
    )(*values, after)


def attention_kernel(heads, blocks, rows, q_ref, kv_ref, after_ref, out_ref, token_ref):
    token_ref[...] = jnp.zeros(token_ref.shape, F32)
    exp = lax.axis_size("exp")
    ctx = lax.axis_size("ctx")
    z = lax.axis_index("exp")
    q = q_ref[...].reshape(blocks * rows, heads * HEAD_WIDTH)
    query = jnp.concatenate(
        [q[:, h * HEAD_WIDTH : (h + 1) * HEAD_WIDTH] for h in range(heads)], axis=0
    )
    scores = lax.dot_general(
        query, kv_ref[:, :HEAD_WIDTH], (((1,), (1,)), ((), ())), preferred_element_type=F32
    ) * (1.0 / math.sqrt(HEAD_WIDTH))
    shape = (1, scores.shape[1])
    place = lax.broadcasted_iota(jnp.int32, shape, 1)
    block = place // rows
    position = ((block % ctx) * exp + ((block // ctx) ^ z)) * rows + place % rows
    shape = (scores.shape[0], 1)
    row = lax.broadcasted_iota(jnp.int32, shape, 0) % (blocks * rows)
    query_block = pl.program_id(0) * blocks + row // rows
    query_position = (query_block * exp + z) * rows + row % rows
    scores = jnp.where(position <= query_position, scores, -1e30)
    row_max = jnp.max(scores, axis=1, keepdims=True)
    probs = jnp.exp(scores - row_max).astype(BF16)
    total = jnp.sum(probs.astype(F32), axis=1, keepdims=True)
    summed = jnp.dot(probs, kv_ref[:, HEAD_WIDTH:], preferred_element_type=F32)
    result = (summed / total).astype(BF16)
    here = blocks * rows
    out_ref[...] = jnp.concatenate(
        [result[h * here : (h + 1) * here] for h in range(heads)], axis=1
    ).reshape(out_ref.shape)


def attend(queries, line, after):
    ctx, rows, width = queries.shape
    blocks = max(1, ctx // 4)
    return pl.pallas_call(
        functools.partial(attention_kernel, width // HEAD_WIDTH, blocks, rows),
        grid=(ctx // blocks,),
        in_specs=[
            pl.BlockSpec((blocks, rows, width), lambda g: (g, 0, 0)),
            pl.BlockSpec(line.shape, lambda g: (0, 0)),
            ANYWHERE,
        ],
        out_specs=[pl.BlockSpec((blocks, rows, width), lambda g: (g, 0, 0)), TOKEN],
        out_shape=[jax.ShapeDtypeStruct(queries.shape, BF16), TOKEN_SHAPE],
        compiler_params=PARAMS,
        cost_estimate=cost("attend"),
    )(queries, line, after)


def slot_matrix(meta_ref, plan, weighted, relative=False):
    places, capacity, top, rows = plan
    tokens = meta_ref.shape[1]
    z, exp = lax.axis_index("exp"), lax.axis_size("exp")
    ids = meta_ref[:top]
    weights = meta_ref[top:]
    members, scales = [], []
    here = lax.axis_index("ctx") if relative else 0
    for m in range(places):
        hit = ids == ((here ^ m) * exp + z).astype(F32)
        members.append(jnp.sum(jnp.where(hit, 1.0, 0.0), axis=0, keepdims=True))
        scales.append(jnp.sum(jnp.where(hit, weights, 0.0), axis=0, keepdims=True))
    member = jnp.concatenate(members, axis=0)
    first = lax.broadcasted_iota(jnp.int32, (tokens, tokens), 0)
    second = lax.broadcasted_iota(jnp.int32, (tokens, tokens), 1)
    before = jnp.where(first < second, 1.0, 0.0).astype(BF16)
    rank = jnp.dot(member.astype(BF16), before, preferred_element_type=F32)
    rank = jnp.where(member > 0.5, rank, -1.0).astype(jnp.int32)
    slot = lax.broadcasted_iota(jnp.int32, (rows, tokens), 0)
    return jnp.concatenate(
        [
            jnp.where(slot == rank[m : m + 1], scales[m] if weighted else 1.0, 0.0)
            for m in range(places)
        ],
        axis=0,
    )


def pack_kernel(plan, count, other, rides, meta_ref, after_ref, arrived_ref, *refs):
    pieces, refs = refs[:count], refs[count:]
    block = jnp.concatenate([ref[...] for ref in pieces], axis=0)
    held = block
    if other:
        held, refs = refs[0][...], refs[1:]
    if rides:
        rider, refs = refs[0][...].astype(F32), refs[1:]
    out_ref, token_ref, *copies, pick_ref = refs
    token_ref[...] = jnp.zeros(token_ref.shape, F32)

    @pl.when(pl.program_id(0) == 0)
    def _():
        pick_ref[...] = slot_matrix(meta_ref, plan, False).astype(BF16)

    packed = jnp.dot(pick_ref[...], block, preferred_element_type=F32)
    if rides:
        places, rows = plan[0], plan[3]
        extra = rider.shape[0] // places
        parts = []
        for m in range(places):
            parts += [packed[m * rows : (m + 1) * rows], rider[m * extra : (m + 1) * extra]]
        packed = jnp.concatenate(parts, axis=0)
    out_ref[...] = packed.astype(BF16)
    start = 0
    for ref in copies:
        ref[...] = held[start % held.shape[0] :][: ref.shape[0]]
        start += ref.shape[0]


def pack(stage, meta, pieces, after, arrived, other, cuts, rider, plan):
    places, capacity, top, rows = plan
    tokens, width = meta.shape[1], pieces[0].shape[1]
    columns = width // 4

    def tile(size):
        return pl.BlockSpec((size, columns), lambda i: (0, i))

    operands = [meta, after, arrived, *pieces]
    in_specs = [pl.BlockSpec(meta.shape, lambda i: (0, 0)), ANYWHERE, ANYWHERE]
    in_specs += [tile(piece.shape[0]) for piece in pieces]
    if other is not None:
        operands.append(other)
        in_specs.append(tile(tokens))
    slots = places * rows
    if rider is not None:
        operands.append(rider)
        in_specs.append(tile(rider.shape[0]))
        slots += rider.shape[0]
    out_specs = [tile(slots), TOKEN] + [tile(size) for size in cuts]
    out_shape = [jax.ShapeDtypeStruct((slots, width), BF16), TOKEN_SHAPE]
    out_shape += [jax.ShapeDtypeStruct((size, width), BF16) for size in cuts]
    return pl.pallas_call(
        functools.partial(
            pack_kernel, plan, len(pieces), other is not None, rider is not None
        ),
        grid=(width // columns,),
        in_specs=in_specs,
        out_specs=out_specs,
        out_shape=out_shape,
        scratch_shapes=[pltpu.VMEM((places * rows, tokens), BF16)],
        compiler_params=PARAMS,
        cost_estimate=cost(f"pack{stage}"),
    )(*operands)


def ffn_kernel(split, x_ref, gate_ref, up_ref, down_ref, after_ref, *refs):
    *outs, token_ref, total_ref = refs
    token_ref[...] = jnp.zeros(token_ref.shape, F32)
    step, last = pl.program_id(0), pl.num_programs(0) - 1
    x = x_ref[...]
    gated = jnp.dot(x, gate_ref[0], preferred_element_type=F32)
    up = jnp.dot(x, up_ref[0], preferred_element_type=F32)
    hidden = (gated / (1.0 + jnp.exp(-gated)) * up).astype(BF16)
    term = jnp.dot(hidden, down_ref[0], preferred_element_type=F32)

    @pl.when(step == 0)
    def _():
        total_ref[...] = term

    @pl.when((step > 0) & (step < last))
    def _():
        total_ref[...] += term

    @pl.when(step == last)
    def _():
        if not split:
            outs[0][...] = (total_ref[...] + term).astype(BF16)
        else:
            total_ref[...] += term
            rows = outs[0].shape[0]
            stride = total_ref.shape[0] // len(outs)
            for m, out_ref in enumerate(outs):
                start = pl.multiple_of((lax.axis_index("ctx") ^ m) * stride, 8)
                out_ref[...] = total_ref[pl.ds(start, rows)].astype(BF16)


def ffn(stage, x, w_gate, w_up, w_down, after, split, kept):
    rows, width = x.shape
    hidden = w_gate.shape[2]
    block = 256
    whole = pl.BlockSpec((rows, width), lambda i: (0, 0))
    part = pl.BlockSpec((kept, width), lambda i: (0, 0))
    return pl.pallas_call(
        functools.partial(ffn_kernel, split > 1),
        grid=(hidden // block,),
        in_specs=[
            whole,
            pl.BlockSpec((1, width, block), lambda i: (0, 0, i)),
            pl.BlockSpec((1, width, block), lambda i: (0, 0, i)),
            pl.BlockSpec((1, block, width), lambda i: (0, i, 0)),
            ANYWHERE,
        ],
        out_specs=[part] * split + [TOKEN],
        out_shape=[jax.ShapeDtypeStruct((kept, width), BF16)] * split + [TOKEN_SHAPE],
        scratch_shapes=[pltpu.VMEM((rows, width), F32)],
        compiler_params=PARAMS,
        cost_estimate=cost(f"ffn{stage}"),
    )(x, w_gate, w_up, w_down, after)


def combine_kernel(plan, backs, count, meta_ref, after_ref, *refs):
    back_refs, pieces, refs = refs[:backs], refs[backs : backs + count], refs[backs + count :]
    outs, (token_ref, high_ref, low_ref) = refs[:-3], refs[-3:]
    token_ref[...] = jnp.zeros(token_ref.shape, F32)

    @pl.when(pl.program_id(0) == 0)
    def _():
        scale = slot_matrix(meta_ref, plan, True, backs > 1)
        high = scale.astype(BF16)
        high_ref[...] = high
        low_ref[...] = (scale - high.astype(F32)).astype(BF16)

    back = back_refs[0][...]
    if backs > 1:
        parts = [ref[...].astype(F32) for ref in back_refs]
        back = jnp.concatenate(parts, axis=0).astype(BF16)
    contract = (((0,), (0,)), ((), ()))
    mixed = lax.dot_general(high_ref[...], back, contract, preferred_element_type=F32)
    mixed = mixed + lax.dot_general(low_ref[...], back, contract, preferred_element_type=F32)
    if count:
        mixed = mixed + jnp.concatenate([ref[...] for ref in pieces], axis=0).astype(F32)
    rows = outs[0].shape[0]
    for index, ref in enumerate(outs):
        ref[...] = mixed[index * rows : (index + 1) * rows].astype(ref.dtype)


def combine(stage, meta, backs, after, pieces, outs, dtype, plan):
    tokens = meta.shape[1]
    width = backs[0].shape[1]
    slots = plan[0] * plan[3]
    columns = width // 4

    def tile(size):
        return pl.BlockSpec((size, columns), lambda i: (0, i))

    return pl.pallas_call(
        functools.partial(combine_kernel, plan, len(backs), len(pieces)),
        grid=(width // columns,),
        in_specs=[pl.BlockSpec(meta.shape, lambda i: (0, 0)), ANYWHERE]
        + [tile(piece.shape[0]) for piece in [*backs, *pieces]],
        out_specs=[tile(tokens // outs)] * outs + [TOKEN],
        out_shape=[jax.ShapeDtypeStruct((tokens // outs, width), dtype)] * outs + [TOKEN_SHAPE],
        scratch_shapes=[pltpu.VMEM((slots, tokens), BF16)] * 2,
        compiler_params=PARAMS,
        cost_estimate=cost(f"combine{stage}"),
    )(meta, after, *backs, *pieces)


def finish_kernel(pieces, own_ref, *refs):
    out_ref = refs[-1]
    parts = [jnp.concatenate([refs[i][...] for i in group], axis=0) for group in pieces]
    total = own_ref[...]
    for part in parts:
        total = total + part.astype(F32)
    out_ref[...] = total.astype(BF16)


def finish(own, parts):
    tokens, width = own.shape
    columns = width // 4
    tile = pl.BlockSpec((tokens, columns), lambda i: (0, i))
    flat = [piece for part in parts for piece in part]
    pieces, start = [], 0
    for part in parts:
        pieces.append(range(start, start + len(part)))
        start += len(part)
    return pl.pallas_call(
        functools.partial(finish_kernel, pieces),
        grid=(width // columns,),
        in_specs=[tile]
        + [pl.BlockSpec((piece.shape[0], columns), lambda i: (0, i)) for piece in flat],
        out_specs=tile,
        out_shape=jax.ShapeDtypeStruct(own.shape, BF16),
        compiler_params=PARAMS,
        cost_estimate=cost("finish"),
    )(own, *flat)


def body(queries, keys, values, moe_rows, expert_ids, route_weights, w_gate, w_up, w_down):
    ctx, exp = lax.axis_size("ctx"), lax.axis_size("exp")
    sequence, query_width = queries.shape
    kv_heads = keys.shape[1] // HEAD_WIDTH
    tokens, width = moe_rows.shape
    top = expert_ids.shape[1]
    capacity = max(2, tokens * top * 5 // (4 * ctx * exp))
    rows = -(-capacity // 8) * 8
    plan = (ctx, capacity, top, rows)

    meta = jnp.concatenate([expert_ids.astype(F32).T, route_weights.T], axis=0)
    metas = [meta] + [swap(meta, "exp", s) for s in range(1, exp)]
    state = {"after": sum(metas[1:])[:8]}
    sent, served, partial, arrived = {}, {}, {}, {0: [moe_rows]}

    def mark(value):
        return value.reshape(-1, value.shape[-1])[:8, :128].astype(F32)

    q = queries.reshape(sequence, ctx, query_width // ctx).transpose(1, 0, 2)
    k = keys.reshape(sequence, kv_heads, HEAD_WIDTH).transpose(1, 0, 2)
    v = values.reshape(sequence, kv_heads, HEAD_WIDTH).transpose(1, 0, 2)
    kv = jnp.repeat(jnp.concatenate([k, v], axis=2), ctx // kv_heads, axis=0)
    rider = jnp.concatenate([q, kv], axis=2)
    flat = rider.size // (ctx * width)
    extra = -(-flat // 16) * 16
    rider = jnp.pad(rider.reshape(ctx, flat, width), ((0, 0), (0, extra - flat), (0, 0)))
    rider = rider.reshape(ctx * extra, width)

    halves = [tokens // 2] * 2
    mine = [moe_rows[: tokens // 2], moe_rows[tokens // 2 :]]
    for s in range(1, min(exp, 3)):
        arrived[s] = [swap(piece, "exp", s) for piece in mine]

    def dispatch(s, after):
        other, cuts = (moe_rows, halves) if s == 1 else (None, [])
        result = pack(
            s, metas[s], arrived[s], state["after"], after, other, cuts, rider if s == 1 else None, plan
        )
        if s == 1:
            for t in range(3, exp):
                arrived[t] = [swap(piece, "exp", t) for piece in result[2:]]
        sent[s] = exchange(result[0].reshape(ctx, -1, width))
        state["after"] = result[1]

    def serve(s):
        x = sent[s].reshape(-1, width)
        split, kept = (ctx, rows) if s == 1 else (1, ctx * rows)
        *outs, state["after"] = ffn(s, x, w_gate, w_up, w_down, state["after"], split, kept)
        served[s] = outs[0]
        if s == 1:
            served[s] = outs

    def pass_on(name, group, after):
        values = [served[1][m] for m in group]
        if after is not None:
            values = gate(name, values, after)
        for m, value in zip(group, values):
            served[1][m] = swap(value, "ctx", m)

    def passed(group):
        state["after"] = state["after"] + sum(mark(served[1][m]) for m in group)

    def give_back(s, before):
        out = served[s] if before is None else gate(f"back{s}", [served[s]], before)[0]
        served[s] = exchange(out.reshape(ctx, rows, width))

    def collect(s):
        backs = served[s] if s == 1 else [served[s].reshape(ctx * rows, width)]
        outs, dtype = (1, F32) if s == 0 else (1, BF16) if s == 1 else (2, BF16)
        pieces = partial[2] if s == 0 else []
        *parts, state["after"] = combine(
            s, metas[s], backs, state["after"], pieces, outs, dtype, plan
        )
        partial[s] = parts if s == 0 else [swap(part, "exp", s) for part in parts]

    third = max(1, ctx // 4)
    groups = [range(1, 1 + third), range(1 + third, 1 + 2 * third), range(1 + 2 * third, ctx)]
    dispatch(0, state["after"])
    dispatch(1, state["after"])
    heads = sent[1][:, rows : rows + flat].reshape(ctx, sequence, -1)
    local_queries = heads[:, :, : query_width // ctx]
    local_kv = heads[:, :, query_width // ctx :].reshape(ctx * sequence, 2 * HEAD_WIDTH)
    serve(0)
    dispatch(2, state["after"])
    serve(1)
    pass_on("pass0", groups[0], None)
    for s in range(3, exp):
        dispatch(s, state["after"])
    (held_kv,) = gate("kv", [local_kv], state["after"])
    line = jnp.concatenate([held_kv] + [swap(held_kv, "exp", s) for s in range(1, exp)], axis=0)
    state["after"] = mark(held_kv)
    serve(2)
    pass_on("pass1", groups[1], state["after"])
    passed(groups[0])
    order = list(range(2, exp)) + [0]
    give_back(2, None)
    attended, state["after"] = attend(local_queries, line, state["after"])
    passed(groups[1])
    pass_on("pass2", groups[2], state["after"])
    for s in range(3, exp):
        serve(s)
    for s in range(3, exp):
        give_back(s, mark(served[s - 1]))
    collect(2)
    give_back(0, mark(served[exp - 1]))
    collect(1)
    for s in range(3, exp):
        collect(s)
    collect(0)
    (attended,) = gate("out", [attended], mark(served[0]))
    output = exchange(attended).transpose(1, 0, 2).reshape(sequence, query_width)
    return (output, finish(partial[0][0], [partial[s] for s in [1, *range(3, exp)]]))


def solution(mesh):
    row = P(("ctx", "exp"), None)
    cube = P(("ctx", "exp"), None, None)
    return jax.shard_map(
        body,
        mesh=mesh,
        in_specs=(row,) * 6 + (cube,) * 3,
        out_specs=(row, row),
        check_vma=False,
    )
```

```python
import functools
import math

import jax
import jax.numpy as jnp
from jax import lax
from jax.experimental import pallas as pl
from jax.experimental.pallas import tpu as pltpu
from jax.sharding import PartitionSpec as P

HEAD_WIDTH = 128
F32 = jnp.float32
BF16 = jnp.bfloat16
VMEM = 48 * 1024 * 1024
COSTS = {"pack1": 20, "pack2": 30, "pack3": 20, "ffn2": 15, "ffn3": 20}
COSTS.update({f"combine{s}": 40 for s in range(4)})


def cost(name):
    work = 1024 + int(COSTS.get(name, 0.0) * 1.0e9)
    return pl.CostEstimate(flops=work, bytes_accessed=1024, transcendentals=0)


PARAMS = pltpu.CompilerParams(vmem_limit_bytes=VMEM)
ANYWHERE = pl.BlockSpec(memory_space=pl.ANY)
TOKEN = pl.BlockSpec((8, 128), lambda *step: (0, 0))
TOKEN_SHAPE = jax.ShapeDtypeStruct((8, 128), F32)


def swap(value, axis, offset):
    count = lax.axis_size(axis)
    return lax.ppermute(value, axis, [(i, i ^ offset) for i in range(count)])


def exchange(value):
    return lax.all_to_all(value, "ctx", split_axis=0, concat_axis=0, tiled=True)


def gate(name, values, after):
    return pl.pallas_call(
        lambda *refs: None,
        in_specs=[ANYWHERE] * (len(values) + 1),
        out_specs=[ANYWHERE] * len(values),
        out_shape=[jax.ShapeDtypeStruct(value.shape, value.dtype) for value in values],
        input_output_aliases={i: i for i in range(len(values))},
        cost_estimate=cost(name),
    )(*values, after)


def attention_kernel(heads, blocks, rows, q_ref, kv_ref, after_ref, out_ref, token_ref):
    token_ref[...] = jnp.zeros(token_ref.shape, F32)
    exp = lax.axis_size("exp")
    ctx = lax.axis_size("ctx")
    z = lax.axis_index("exp")
    q = q_ref[...].reshape(blocks * rows, heads * HEAD_WIDTH)
    query = jnp.concatenate(
        [q[:, h * HEAD_WIDTH : (h + 1) * HEAD_WIDTH] for h in range(heads)], axis=0
    )
    scores = lax.dot_general(
        query, kv_ref[:, :HEAD_WIDTH], (((1,), (1,)), ((), ())), preferred_element_type=F32
    ) * (1.0 / math.sqrt(HEAD_WIDTH))
    shape = (1, scores.shape[1])
    place = lax.broadcasted_iota(jnp.int32, shape, 1)
    block = place // rows
    position = ((block % ctx) * exp + ((block // ctx) ^ z)) * rows + place % rows
    shape = (scores.shape[0], 1)
    row = lax.broadcasted_iota(jnp.int32, shape, 0) % (blocks * rows)
    query_block = pl.program_id(0) * blocks + row // rows
    query_position = (query_block * exp + z) * rows + row % rows
    scores = jnp.where(position <= query_position, scores, -1e30)
    row_max = jnp.max(scores, axis=1, keepdims=True)
    probs = jnp.exp(scores - row_max).astype(BF16)
    total = jnp.sum(probs.astype(F32), axis=1, keepdims=True)
    summed = jnp.dot(probs, kv_ref[:, HEAD_WIDTH:], preferred_element_type=F32)
    result = (summed / total).astype(BF16)
    here = blocks * rows
    out_ref[...] = jnp.concatenate(
        [result[h * here : (h + 1) * here] for h in range(heads)], axis=1
    ).reshape(out_ref.shape)


def attend(queries, line, after):
    ctx, rows, width = queries.shape
    blocks = max(1, ctx // 4)
    return pl.pallas_call(
        functools.partial(attention_kernel, width // HEAD_WIDTH, blocks, rows),
        grid=(ctx // blocks,),
        in_specs=[
            pl.BlockSpec((blocks, rows, width), lambda g: (g, 0, 0)),
            pl.BlockSpec(line.shape, lambda g: (0, 0)),
            ANYWHERE,
        ],
        out_specs=[pl.BlockSpec((blocks, rows, width), lambda g: (g, 0, 0)), TOKEN],
        out_shape=[jax.ShapeDtypeStruct(queries.shape, BF16), TOKEN_SHAPE],
        compiler_params=PARAMS,
        cost_estimate=cost("attend"),
    )(queries, line, after)


def slot_matrix(meta_ref, plan, weighted, relative=False):
    places, capacity, top, rows = plan
    tokens = meta_ref.shape[1]
    z, exp = lax.axis_index("exp"), lax.axis_size("exp")
    ids = meta_ref[:top]
    weights = meta_ref[top:]
    members, scales = [], []
    here = lax.axis_index("ctx") if relative else 0
    for m in range(places):
        hit = ids == ((here ^ m) * exp + z).astype(F32)
        members.append(jnp.sum(jnp.where(hit, 1.0, 0.0), axis=0, keepdims=True))
        scales.append(jnp.sum(jnp.where(hit, weights, 0.0), axis=0, keepdims=True))
    member = jnp.concatenate(members, axis=0)
    first = lax.broadcasted_iota(jnp.int32, (tokens, tokens), 0)
    second = lax.broadcasted_iota(jnp.int32, (tokens, tokens), 1)
    before = jnp.where(first < second, 1.0, 0.0).astype(BF16)
    rank = jnp.dot(member.astype(BF16), before, preferred_element_type=F32)
    rank = jnp.where(member > 0.5, rank, -1.0).astype(jnp.int32)
    slot = lax.broadcasted_iota(jnp.int32, (rows, tokens), 0)
    return jnp.concatenate(
        [
            jnp.where(slot == rank[m : m + 1], scales[m] if weighted else 1.0, 0.0)
            for m in range(places)
        ],
        axis=0,
    )


def pack_kernel(plan, count, other, rides, meta_ref, after_ref, arrived_ref, *refs):
    pieces, refs = refs[:count], refs[count:]
    block = jnp.concatenate([ref[...] for ref in pieces], axis=0)
    held = block
    if other:
        held, refs = refs[0][...], refs[1:]
    if rides:
        rider, refs = refs[0][...].astype(F32), refs[1:]
    out_ref, token_ref, *copies, pick_ref = refs
    token_ref[...] = jnp.zeros(token_ref.shape, F32)

    @pl.when(pl.program_id(0) == 0)
    def _():
        pick_ref[...] = slot_matrix(meta_ref, plan, False).astype(BF16)

    packed = jnp.dot(pick_ref[...], block, preferred_element_type=F32)
    if rides:
        places, rows = plan[0], plan[3]
        extra = rider.shape[0] // places
        parts = []
        for m in range(places):
            parts += [packed[m * rows : (m + 1) * rows], rider[m * extra : (m + 1) * extra]]
        packed = jnp.concatenate(parts, axis=0)
    out_ref[...] = packed.astype(BF16)
    start = 0
    for ref in copies:
        ref[...] = held[start % held.shape[0] :][: ref.shape[0]]
        start += ref.shape[0]


def pack(stage, meta, pieces, after, arrived, other, cuts, rider, plan):
    places, capacity, top, rows = plan
    tokens, width = meta.shape[1], pieces[0].shape[1]
    columns = width // 4

    def tile(size):
        return pl.BlockSpec((size, columns), lambda i: (0, i))

    operands = [meta, after, arrived, *pieces]
    in_specs = [pl.BlockSpec(meta.shape, lambda i: (0, 0)), ANYWHERE, ANYWHERE]
    in_specs += [tile(piece.shape[0]) for piece in pieces]
    if other is not None:
        operands.append(other)
        in_specs.append(tile(tokens))
    slots = places * rows
    if rider is not None:
        operands.append(rider)
        in_specs.append(tile(rider.shape[0]))
        slots += rider.shape[0]
    out_specs = [tile(slots), TOKEN] + [tile(size) for size in cuts]
    out_shape = [jax.ShapeDtypeStruct((slots, width), BF16), TOKEN_SHAPE]
    out_shape += [jax.ShapeDtypeStruct((size, width), BF16) for size in cuts]
    return pl.pallas_call(
        functools.partial(
            pack_kernel, plan, len(pieces), other is not None, rider is not None
        ),
        grid=(width // columns,),
        in_specs=in_specs,
        out_specs=out_specs,
        out_shape=out_shape,
        scratch_shapes=[pltpu.VMEM((places * rows, tokens), BF16)],
        compiler_params=PARAMS,
        cost_estimate=cost(f"pack{stage}"),
    )(*operands)


def ffn_kernel(split, x_ref, gate_ref, up_ref, down_ref, after_ref, *refs):
    *outs, token_ref, total_ref = refs
    token_ref[...] = jnp.zeros(token_ref.shape, F32)
    step, last = pl.program_id(0), pl.num_programs(0) - 1
    x = x_ref[...]
    gated = jnp.dot(x, gate_ref[0], preferred_element_type=F32)
    up = jnp.dot(x, up_ref[0], preferred_element_type=F32)
    hidden = (gated / (1.0 + jnp.exp(-gated)) * up).astype(BF16)
    term = jnp.dot(hidden, down_ref[0], preferred_element_type=F32)

    @pl.when(step == 0)
    def _():
        total_ref[...] = term

    @pl.when((step > 0) & (step < last))
    def _():
        total_ref[...] += term

    @pl.when(step == last)
    def _():
        if not split:
            outs[0][...] = (total_ref[...] + term).astype(BF16)
        else:
            total_ref[...] += term
            rows = outs[0].shape[0]
            stride = total_ref.shape[0] // len(outs)
            for m, out_ref in enumerate(outs):
                start = pl.multiple_of((lax.axis_index("ctx") ^ m) * stride, 8)
                out_ref[...] = total_ref[pl.ds(start, rows)].astype(BF16)


def ffn(stage, x, w_gate, w_up, w_down, after, split, kept):
    rows, width = x.shape
    hidden = w_gate.shape[2]
    block = 256
    whole = pl.BlockSpec((rows, width), lambda i: (0, 0))
    part = pl.BlockSpec((kept, width), lambda i: (0, 0))
    return pl.pallas_call(
        functools.partial(ffn_kernel, split > 1),
        grid=(hidden // block,),
        in_specs=[
            whole,
            pl.BlockSpec((1, width, block), lambda i: (0, 0, i)),
            pl.BlockSpec((1, width, block), lambda i: (0, 0, i)),
            pl.BlockSpec((1, block, width), lambda i: (0, i, 0)),
            ANYWHERE,
        ],
        out_specs=[part] * split + [TOKEN],
        out_shape=[jax.ShapeDtypeStruct((kept, width), BF16)] * split + [TOKEN_SHAPE],
        scratch_shapes=[pltpu.VMEM((rows, width), F32)],
        compiler_params=PARAMS,
        cost_estimate=cost(f"ffn{stage}"),
    )(x, w_gate, w_up, w_down, after)


def combine_kernel(plan, backs, count, meta_ref, after_ref, *refs):
    back_refs, pieces, refs = refs[:backs], refs[backs : backs + count], refs[backs + count :]
    outs, (token_ref, high_ref, low_ref) = refs[:-3], refs[-3:]
    token_ref[...] = jnp.zeros(token_ref.shape, F32)

    @pl.when(pl.program_id(0) == 0)
    def _():
        scale = slot_matrix(meta_ref, plan, True, backs > 1)
        high = scale.astype(BF16)
        high_ref[...] = high
        low_ref[...] = (scale - high.astype(F32)).astype(BF16)

    back = back_refs[0][...]
    if backs > 1:
        parts = [ref[...].astype(F32) for ref in back_refs]
        back = jnp.concatenate(parts, axis=0).astype(BF16)
    contract = (((0,), (0,)), ((), ()))
    mixed = lax.dot_general(high_ref[...], back, contract, preferred_element_type=F32)
    mixed = mixed + lax.dot_general(low_ref[...], back, contract, preferred_element_type=F32)
    if count:
        mixed = mixed + jnp.concatenate([ref[...] for ref in pieces], axis=0).astype(F32)
    rows = outs[0].shape[0]
    for index, ref in enumerate(outs):
        ref[...] = mixed[index * rows : (index + 1) * rows].astype(ref.dtype)


def combine(stage, meta, backs, after, pieces, outs, dtype, plan):
    tokens = meta.shape[1]
    width = backs[0].shape[1]
    slots = plan[0] * plan[3]
    columns = width // 4

    def tile(size):
        return pl.BlockSpec((size, columns), lambda i: (0, i))

    return pl.pallas_call(
        functools.partial(combine_kernel, plan, len(backs), len(pieces)),
        grid=(width // columns,),
        in_specs=[pl.BlockSpec(meta.shape, lambda i: (0, 0)), ANYWHERE]
        + [tile(piece.shape[0]) for piece in [*backs, *pieces]],
        out_specs=[tile(tokens // outs)] * outs + [TOKEN],
        out_shape=[jax.ShapeDtypeStruct((tokens // outs, width), dtype)] * outs + [TOKEN_SHAPE],
        scratch_shapes=[pltpu.VMEM((slots, tokens), BF16)] * 2,
        compiler_params=PARAMS,
        cost_estimate=cost(f"combine{stage}"),
    )(meta, after, *backs, *pieces)


def finish_kernel(pieces, own_ref, *refs):
    out_ref = refs[-1]
    parts = [jnp.concatenate([refs[i][...] for i in group], axis=0) for group in pieces]
    total = own_ref[...]
    for part in parts:
        total = total + part.astype(F32)
    out_ref[...] = total.astype(BF16)


def finish(own, parts):
    tokens, width = own.shape
    columns = width // 4
    tile = pl.BlockSpec((tokens, columns), lambda i: (0, i))
    flat = [piece for part in parts for piece in part]
    pieces, start = [], 0
    for part in parts:
        pieces.append(range(start, start + len(part)))
        start += len(part)
    return pl.pallas_call(
        functools.partial(finish_kernel, pieces),
        grid=(width // columns,),
        in_specs=[tile]
        + [pl.BlockSpec((piece.shape[0], columns), lambda i: (0, i)) for piece in flat],
        out_specs=tile,
        out_shape=jax.ShapeDtypeStruct(own.shape, BF16),
        compiler_params=PARAMS,
        cost_estimate=cost("finish"),
    )(own, *flat)


def body(queries, keys, values, moe_rows, expert_ids, route_weights, w_gate, w_up, w_down):
    ctx, exp = lax.axis_size("ctx"), lax.axis_size("exp")
    sequence, query_width = queries.shape
    kv_heads = keys.shape[1] // HEAD_WIDTH
    tokens, width = moe_rows.shape
    top = expert_ids.shape[1]
    capacity = max(2, tokens * top * 5 // (4 * ctx * exp))
    rows = -(-capacity // 8) * 8
    plan = (ctx, capacity, top, rows)

    meta = jnp.concatenate([expert_ids.astype(F32).T, route_weights.T], axis=0)
    metas = [meta] + [swap(meta, "exp", s) for s in range(1, exp)]
    state = {"after": sum(metas[1:])[:8]}
    sent, served, partial, arrived = {}, {}, {}, {0: [moe_rows]}

    def mark(value):
        return value.reshape(-1, value.shape[-1])[:8, :128].astype(F32)

    q = queries.reshape(sequence, ctx, query_width // ctx).transpose(1, 0, 2)
    k = keys.reshape(sequence, kv_heads, HEAD_WIDTH).transpose(1, 0, 2)
    v = values.reshape(sequence, kv_heads, HEAD_WIDTH).transpose(1, 0, 2)
    kv = jnp.repeat(jnp.concatenate([k, v], axis=2), ctx // kv_heads, axis=0)
    rider = jnp.concatenate([q, kv], axis=2)
    flat = rider.size // (ctx * width)
    extra = -(-flat // 16) * 16
    rider = jnp.pad(rider.reshape(ctx, flat, width), ((0, 0), (0, extra - flat), (0, 0)))
    rider = rider.reshape(ctx * extra, width)

    halves = [tokens // 2] * 2
    mine = [moe_rows[: tokens // 2], moe_rows[tokens // 2 :]]
    for s in range(1, min(exp, 3)):
        arrived[s] = [swap(piece, "exp", s) for piece in mine]

    def dispatch(s, after):
        other, cuts = (moe_rows, halves) if s == 1 else (None, [])
        result = pack(
            s, metas[s], arrived[s], state["after"], after, other, cuts, rider if s == 1 else None, plan
        )
        if s == 1:
            for t in range(3, exp):
                arrived[t] = [swap(piece, "exp", t) for piece in result[2:]]
        sent[s] = exchange(result[0].reshape(ctx, -1, width))
        state["after"] = result[1]

    def serve(s):
        x = sent[s].reshape(-1, width)
        split, kept = (ctx, rows) if s == 1 else (1, ctx * rows)
        *outs, state["after"] = ffn(s, x, w_gate, w_up, w_down, state["after"], split, kept)
        served[s] = outs[0]
        if s == 1:
            served[s] = outs

    def pass_on(name, group, after):
        values = [served[1][m] for m in group]
        if after is not None:
            values = gate(name, values, after)
        for m, value in zip(group, values):
            served[1][m] = swap(value, "ctx", m)

    def passed(group):
        state["after"] = state["after"] + sum(mark(served[1][m]) for m in group)

    def give_back(s, before):
        out = served[s] if before is None else gate(f"back{s}", [served[s]], before)[0]
        served[s] = exchange(out.reshape(ctx, rows, width))

    def collect(s):
        backs = served[s] if s == 1 else [served[s].reshape(ctx * rows, width)]
        outs, dtype = (1, F32) if s == 0 else (1, BF16) if s == 1 else (2, BF16)
        pieces = partial[2] if s == 0 else []
        *parts, state["after"] = combine(
            s, metas[s], backs, state["after"], pieces, outs, dtype, plan
        )
        partial[s] = parts if s == 0 else [swap(part, "exp", s) for part in parts]

    third = max(1, ctx // 4)
    groups = [range(1, 1 + third), range(1 + third, 1 + 2 * third), range(1 + 2 * third, ctx)]
    dispatch(0, state["after"])
    dispatch(1, state["after"])
    heads = sent[1][:, rows : rows + flat].reshape(ctx, sequence, -1)
    local_queries = heads[:, :, : query_width // ctx]
    local_kv = heads[:, :, query_width // ctx :].reshape(ctx * sequence, 2 * HEAD_WIDTH)
    serve(0)
    dispatch(2, state["after"])
    serve(1)
    pass_on("pass0", groups[0], None)
    for s in range(3, exp):
        dispatch(s, state["after"])
    (held_kv,) = gate("kv", [local_kv], state["after"])
    line = jnp.concatenate([held_kv] + [swap(held_kv, "exp", s) for s in range(1, exp)], axis=0)
    state["after"] = mark(held_kv)
    serve(2)
    pass_on("pass1", groups[1], state["after"])
    passed(groups[0])
    order = list(range(2, exp)) + [0]
    give_back(2, None)
    attended, state["after"] = attend(local_queries, line, state["after"])
    passed(groups[1])
    pass_on("pass2", groups[2], state["after"])
    for s in range(3, exp):
        serve(s)
    for s in range(3, exp):
        give_back(s, mark(served[s - 1]))
    collect(2)
    give_back(0, mark(served[exp - 1]))
    collect(1)
    for s in range(3, exp):
        collect(s)
    collect(0)
    (attended,) = gate("out", [attended], mark(served[0]))
    output = exchange(attended).transpose(1, 0, 2).reshape(sequence, query_width)
    return (output, finish(partial[0][0], [partial[s] for s in [1, *range(3, exp)]]))


def solution(mesh):
    row = P(("ctx", "exp"), None)
    cube = P(("ctx", "exp"), None, None)
    return jax.shard_map(
        body,
        mesh=mesh,
        in_specs=(row,) * 6 + (cube,) * 3,
        out_specs=(row, row),
        check_vma=False,
    )
```
